32 devices in a mesh: grp: 2 (over y), row: 4 (over x, core), ch: 4 (over z).
Axes of the slice: x: 2, y: 2, z: 4, core: 2. Of those that a mesh axis runs over, the one named last changes fastest.
Arguments:
- pair_tensor: bfloat16 [512, 256, 128], P(('grp', 'row'), 'ch'), parts along dimension 0, may hold values from -6 to 6
- cotangent: bfloat16 [512, 256, 128], P(('grp', 'row'), 'ch'), parts along dimension 0, may hold values from -6 to 6
- residue_mask: int32 [512], P('grp'), parts along dimension 0, may hold values 0 or 1
- in_gain: float32 [128], replicated, may hold values from 0.1 to 1.9
- edge_weight: bfloat16 [4, 128, 128], replicated, may hold values from -0.5 to 0.5
- gate_weight: bfloat16 [128, 128], replicated, may hold values from -0.5 to 0.5
- out_gain: float32 [128], replicated, may hold values from 0.1 to 1.9
- out_weight: bfloat16 [128, 128], replicated, may hold values from -0.5 to 0.5
Outputs:
- pair_update: bfloat16 [512, 256, 128], P(('grp', 'row'), 'ch'), parts along dimension 0
- grad_pair: bfloat16 [512, 256, 128], P(('grp', 'row'), 'ch'), parts along dimension 0
The draws below stay inside these ranges and needn't reach their ends.
There are 2 independent parts, one for each index of `grp`. The reference program is written for one: setup_inputs(seed, part) draws one part's arguments, and reference() takes and returns one part's arrays. A program takes and returns all parts, laid end to end along the dimension named above; an argument that names none is the same for every part. Nothing has to cross between parts.
Inputs may be any that keep to these rules, and one draw needn't show every extreme that they name: `residue_mask`: 1 marks a residue that is present, 0 a padded one.
All inputs are finite; a program needn't handle non-finite values.
Results may differ from the reference program's by a relative error of at most 0.0086.
Values may be sent and summed in bfloat16 or wider, within the bound.
A program may use at most 192 MiB of HBM per device.

```python
import jax
import jax.numpy as jnp
from jax import lax

C = 128
H = 128
N = 256


def touch_ends(values, rng, smallest, high):
    index_at = [jax.random.randint(jax.random.fold_in(rng, axis), (), 0, length) for axis, length in enumerate(values.shape)]
    longest = values.shape.index(max(values.shape))
    neighbour = index_at[:longest] + [(index_at[longest] + 1) % values.shape[longest]] + index_at[longest + 1:]
    return values.at[tuple(index_at)].set(smallest).at[tuple(neighbour)].set(high)


def shard_levels(stream_key, extent, cuts, low, largest):
    loudness, own = 1.0, jax.random.fold_in(stream_key, 6)
    for axis_at, shards_of in cuts:
        steps = jnp.exp(jax.random.uniform(jax.random.fold_in(own, axis_at), (shards_of,), jnp.float32, low / len(cuts), largest / len(cuts)))
        loudness = loudness * jnp.repeat(steps, extent[axis_at] // shards_of).reshape([-1 if axis == axis_at else 1 for axis in range(len(extent))])
    return loudness


def scatter_about(rng, dims, deviation, most, shards=(), held_as=jnp.bfloat16):
    factor_of = shard_levels(rng, dims, shards, -0.22, 0.18) if shards else 1.0
    values = jax.random.normal(rng, dims, jnp.float32) * deviation * factor_of
    return jnp.minimum(jnp.maximum(values, -most), most).astype(held_as)


def setup_inputs(seed: int = 0, part: int = 0) -> dict:
    key_of = jax.random.split(jax.random.key(seed), 9)
    part_splits = jax.random.split(jax.random.fold_in(key_of[8], part), 9)
    return {
        "pair_tensor": scatter_about(part_splits[0], (N, N, C), 1.0, 6.0, ((0, 4), (1, 4))),
        "cotangent": scatter_about(part_splits[1], (N, N, C), 1.0, 6.0, ((0, 4), (1, 4))),
        "residue_mask": touch_ends((jax.random.randint(part_splits[2], (N,), 0, 16) < 15).astype(jnp.int32), jax.random.fold_in(part_splits[2], 1), 0, 1),
        "in_gain": jnp.clip(1.0 + 0.18 * jax.random.normal(key_of[3], (C,), jnp.float32), 0.1, 1.9),
        "edge_weight": scatter_about(key_of[4], (4, C, H), C ** -0.5, 0.5),
        "gate_weight": scatter_about(key_of[5], (C, C), C ** -0.5, 0.5),
        "out_gain": jnp.clip(1.0 + 0.18 * jax.random.normal(key_of[6], (H,), jnp.float32), 0.1, 1.9),
        "out_weight": scatter_about(key_of[7], (H, C), H ** -0.5, 0.5),
    }


epsilon = 1e-05

def normalize(values, axis):
    mean_val = lax.optimization_barrier(jnp.mean(values, axis=axis, keepdims=True))
    centered = values - mean_val
    variance = lax.optimization_barrier(jnp.mean(centered * centered, axis=axis, keepdims=True))
    inv_scale = lax.rsqrt(variance + epsilon)
    return (centered * inv_scale, inv_scale)

def layer_back(d_hat, hat, inv_scale, axis):
    first = lax.optimization_barrier(jnp.mean(d_hat, axis=axis, keepdims=True))
    second = lax.optimization_barrier(jnp.mean(d_hat * hat, axis=axis, keepdims=True))
    return inv_scale * (d_hat - first - hat * second)

def reference(pair_tensor, cotangent, residue_mask, in_gain, edge_weight, gate_weight, out_gain, out_weight):
    residues = pair_tensor.shape[0]
    channels = pair_tensor.shape[2]
    z_hat, inv_in = normalize(pair_tensor.astype(jnp.float32), -1)
    normed = (z_hat * in_gain).astype(jnp.bfloat16)
    flat = normed.reshape(-1, channels)
    live = residue_mask.astype(jnp.float32)
    pair_mask = (live[:, None] * live[None, :])[..., None]

    def project(index):
        return jnp.dot(flat, edge_weight[index], preferred_element_type=jnp.float32).reshape(residues, residues, -1)
    left_sig = jax.nn.sigmoid(project(0))
    left_val = project(1)
    left = (pair_mask * left_sig * left_val).astype(jnp.bfloat16)
    right_sig = jax.nn.sigmoid(project(2))
    right_val = project(3)
    right = (pair_mask * right_sig * right_val).astype(jnp.bfloat16)
    left_h = jnp.transpose(left, (2, 0, 1)).astype(jnp.float32)
    right_h = jnp.transpose(right, (2, 0, 1)).astype(jnp.float32)
    tri = jnp.einsum('hik,hjk->hij', left_h, right_h).astype(jnp.bfloat16)
    t_hat, inv_tri = normalize(tri.astype(jnp.float32), 0)
    normed_tri = (t_hat * out_gain[:, None, None]).astype(jnp.bfloat16)
    proj_out = jnp.einsum('hij,hc->ijc', normed_tri.astype(jnp.float32), out_weight.astype(jnp.float32))
    gate = jax.nn.sigmoid(jnp.dot(flat, gate_weight, preferred_element_type=jnp.float32).reshape(residues, residues, channels))
    pair_update = (gate * proj_out).astype(jnp.bfloat16)
    grad_in = cotangent.astype(jnp.float32)
    d_out = (grad_in * gate).astype(jnp.bfloat16)
    d_gate = (grad_in * proj_out * gate * (1.0 - gate)).astype(jnp.bfloat16)
    d_ntri = jnp.einsum('ijc,hc->hij', d_out.astype(jnp.float32), out_weight.astype(jnp.float32))
    d_tri = layer_back(d_ntri * out_gain[:, None, None], t_hat, inv_tri, 0).astype(jnp.bfloat16)
    d_tri_f = d_tri.astype(jnp.float32)
    d_left = jnp.einsum('hij,hjk->ikh', d_tri_f, right_h).astype(jnp.bfloat16)
    d_right = jnp.einsum('hij,hik->jkh', d_tri_f, left_h).astype(jnp.bfloat16)
    dl_masked = d_left.astype(jnp.float32) * pair_mask
    dr_masked = d_right.astype(jnp.float32) * pair_mask
    d_projs = [dl_masked * left_val * left_sig * (1.0 - left_sig), dl_masked * left_sig, dr_masked * right_val * right_sig * (1.0 - right_sig), dr_masked * right_sig]
    d_normed = jnp.dot(d_gate.reshape(-1, channels), gate_weight.T, preferred_element_type=jnp.float32)
    for index in range(4):
        term = d_projs[index].astype(jnp.bfloat16).reshape(residues * residues, -1)
        d_normed = d_normed + jnp.dot(term, edge_weight[index].T, preferred_element_type=jnp.float32)
    d_normed = d_normed.reshape(residues, residues, channels)
    grad_pair = layer_back(d_normed * in_gain, z_hat, inv_in, -1).astype(jnp.bfloat16)
    return (pair_update, grad_pair)
```

```python
import functools

import jax
import jax.numpy as jnp
from jax import lax
from jax.experimental import pallas as pl
from jax.experimental.pallas import tpu as pltpu
from jax.sharding import PartitionSpec as P

epsilon = 1e-05


def normalize(values, axis):
    mean_val = jnp.mean(values, axis=axis, keepdims=True)
    centered = values - mean_val
    variance = jnp.mean(centered * centered, axis=axis, keepdims=True)
    inv_scale = lax.rsqrt(variance + epsilon)
    return (centered * inv_scale, inv_scale)


def layer_back(d_hat, hat, inv_scale, axis):
    first = jnp.mean(d_hat, axis=axis, keepdims=True)
    second = jnp.mean(d_hat * hat, axis=axis, keepdims=True)
    return inv_scale * (d_hat - first - hat * second)


def per_device(
    pair_tensor, cotangent, residue_mask, in_gain, edge_weight, gate_weight, out_gain, out_weight
):
    row_count = pair_tensor.shape[0]
    col_count = pair_tensor.shape[1]
    row_start = lax.axis_index("row") * row_count
    col_start = lax.axis_index("ch") * col_count
    live = residue_mask.astype(jnp.float32)
    live_rows = lax.dynamic_slice_in_dim(live, row_start, row_count)
    live_cols = lax.dynamic_slice_in_dim(live, col_start, col_count)
    pair_mask = live_rows[:, None] * live_cols[None, :]
    z_hat, inv_in = normalize(pair_tensor.astype(jnp.float32), -1)
    normed = (z_hat * in_gain).astype(jnp.bfloat16)
    proj = jnp.einsum("rjc,tch->thrj", normed, edge_weight, preferred_element_type=jnp.float32)
    shape_four = proj.shape
    proj_pairs = proj.reshape(2, 2, shape_four[1], row_count, col_count)
    edge_sig = jax.nn.sigmoid(proj_pairs[:, 0])
    edge_val = proj_pairs[:, 1]
    edges = (pair_mask * edge_sig * edge_val).astype(jnp.bfloat16)
    edge_chan = lax.all_to_all(edges, "ch", split_axis=1, concat_axis=3, tiled=True)
    left_c = edge_chan[0]
    right_c = edge_chan[1]
    shard_piece = lax.all_gather(right_c, "row", axis=1, tiled=True)
    block = jnp.einsum("hik,hjk->hij", left_c, shard_piece, preferred_element_type=jnp.float32)
    kept = shard_piece
    tri_full, kept = (block, kept)
    tri = tri_full.astype(jnp.bfloat16)
    tri_home = lax.all_to_all(tri, "ch", split_axis=2, concat_axis=0, tiled=True)
    t_hat, inv_tri = normalize(tri_home.astype(jnp.float32), 0)
    normed_tri = (t_hat * out_gain[:, None, None]).astype(jnp.bfloat16)
    proj_out = jnp.einsum("hrj,hc->rjc", normed_tri, out_weight, preferred_element_type=jnp.float32)
    gate = jax.nn.sigmoid(
        jnp.einsum("rjc,cd->rjd", normed, gate_weight, preferred_element_type=jnp.float32)
    )
    pair_update = (gate * proj_out).astype(jnp.bfloat16)
    grad_in = cotangent.astype(jnp.float32)
    d_out = (grad_in * gate).astype(jnp.bfloat16)
    d_gate = (grad_in * proj_out * gate * (1.0 - gate)).astype(jnp.bfloat16)
    d_ntri = jnp.einsum("rjc,hc->hrj", d_out, out_weight, preferred_element_type=jnp.float32)
    d_tri = layer_back(d_ntri * out_gain[:, None, None], t_hat, inv_tri, 0).astype(jnp.bfloat16)
    d_tri_c = lax.all_to_all(d_tri, "ch", split_axis=0, concat_axis=2, tiled=True)
    d_tri_t = lax.all_to_all(d_tri_c, "row", split_axis=2, concat_axis=1, tiled=True)
    d_left = jnp.einsum("hij,hjk->hik", d_tri_c, kept, preferred_element_type=jnp.float32)
    d_right = jnp.einsum(
        "hij,hik->hjk",
        d_tri_t,
        lax.all_gather(left_c, "row", axis=1, tiled=True),
        preferred_element_type=jnp.float32,
    )
    edge_grads = jnp.stack([d_left, d_right]).astype(jnp.bfloat16)
    grads_home = lax.all_to_all(edge_grads, "ch", split_axis=3, concat_axis=1, tiled=True)
    d_masked = grads_home.astype(jnp.float32) * pair_mask
    d_gates = d_masked * edge_val * edge_sig * (1.0 - edge_sig)
    d_values = d_masked * edge_sig
    d_proj = jnp.stack([d_gates, d_values], axis=1).reshape(shape_four).astype(jnp.bfloat16)
    d_normed = jnp.einsum("thrj,tch->rjc", d_proj, edge_weight, preferred_element_type=jnp.float32)
    d_normed = d_normed + jnp.einsum(
        "rjd,cd->rjc", d_gate, gate_weight, preferred_element_type=jnp.float32
    )
    grad_pair = layer_back(d_normed * in_gain, z_hat, inv_in, -1).astype(jnp.bfloat16)
    return (pair_update, grad_pair)


GROUP = 4
TILE = 16


def dot(a, b, dims):
    return lax.dot_general(a, b, ((dims[:1], dims[1:]), ((), ())), preferred_element_type=jnp.float32)


def fused_kernel(
    rows_n, chs_n,
    x_ref, cot_ref, mask_ref, gin_ref, wt_ref, gw_ref, gout_ref, ow_ref,
    update_ref, grad_ref,
    hat_ref, inv_ref, gate_ref, dgate_ref, slope_ref, msig_ref,
    flip_ref, tri_ref, back_ref, left_ref, right_ref, d_full_ref,
    send_e, recv_e, send_t, recv_t, send_d, recv_d, send_g, recv_g,
    send_sem, recv_sem,
):
    f32, bf16 = jnp.float32, jnp.bfloat16
    peers = rows_n * chs_n
    rows, cols, chans = x_ref.shape
    half = rows // 2
    lanes = 2 * cols
    hidden = ow_ref.shape[0]
    own_h = hidden // peers
    part_h = own_h // 2
    chunks = half // TILE
    wide = GROUP * lanes
    groups = TILE // GROUP
    me = lax.axis_index("row") * chs_n + lax.axis_index("ch")

    def device(flat):
        return {"row": flat // chs_n, "ch": lax.rem(flat, chs_n)}

    def make_copy(phase, chunk, offset, send, recv, target, slot):
        return pltpu.make_async_remote_copy(
            src_ref=send.at[chunk, target],
            dst_ref=recv.at[chunk, slot],
            send_sem=send_sem.at[phase, chunk, offset],
            recv_sem=recv_sem.at[phase, chunk, offset],
            device_id=device(target),
            device_id_type=pl.DeviceIdType.MESH,
        )

    def start_all(phase, chunk, send, recv, fill):
        def step(offset, carry):
            target = lax.rem(me + offset, peers)
            if fill is not None:
                send[chunk, target] = fill(target)
            make_copy(phase, chunk, offset, send, recv, target, me).start()
            return carry

        lax.fori_loop(1, peers, step, 0)
        if fill is None:
            recv[chunk, me] = send[chunk, me]
        else:
            recv[chunk, me] = fill(me)

    def wait_all(phase, chunk, send, recv, use):
        if use is not None:
            use(me)

        def step(offset, carry):
            target = lax.rem(me + offset, peers)
            origin = lax.rem(me - offset + peers, peers)
            make_copy(phase, chunk, offset, send, recv, target, origin).wait_recv()
            if use is not None:
                use(origin)
            return carry

        lax.fori_loop(1, peers, step, 0)

    def wait_sends(phase, chunk, send, recv):
        def step(offset, carry):
            target = lax.rem(me + offset, peers)
            make_copy(phase, chunk, offset, send, recv, target, me).wait_send()
            return carry

        lax.fori_loop(1, peers, step, 0)

    def pairs_of(ref, first):
        low = ref[pl.ds(first, GROUP)]
        high = ref[pl.ds(first + half, GROUP)]
        return jnp.concatenate([low, high], axis=1).reshape(wide, chans)

    def put_pairs(ref, first, values):
        values = values.reshape(GROUP, lanes, chans)
        ref[pl.ds(first, GROUP)] = values[:, :cols]
        ref[pl.ds(first + half, GROUP)] = values[:, cols:]

    barrier = pltpu.get_barrier_semaphore()

    def greet(offset, carry):
        pl.semaphore_signal(
            barrier, inc=1, device_id=device(lax.rem(me + offset, peers)),
            device_id_type=pl.DeviceIdType.MESH,
        )
        return carry

    lax.fori_loop(1, peers, greet, 0)

    for chunk in range(chunks):

        def project(step, carry):
            first = chunk * TILE + step * GROUP
            block = chunk * groups + step
            at = pl.ds(pl.multiple_of(block * wide, wide), wide)
            x = pairs_of(x_ref, first).astype(f32)
            centered = x - jnp.mean(x, axis=-1, keepdims=True)
            inv = lax.rsqrt(jnp.mean(centered * centered, axis=-1, keepdims=True) + epsilon)
            hat = centered * inv
            hat_ref[at, :] = hat
            inv_ref[at, :] = jnp.broadcast_to(inv, (wide, chans))
            normed = (hat * gin_ref[...]).astype(bf16)
            gate_ref[at, :] = jax.nn.sigmoid(dot(normed, gw_ref[...], (1, 0)))
            mask = jnp.concatenate([mask_ref[pl.ds(first + s, 1), :] for s in range(GROUP)], axis=1)
            for side in range(2):
                proj = dot(wt_ref[pl.ds(2 * side * hidden, 2 * hidden), :], normed, (1, 1))
                sig = jax.nn.sigmoid(proj[:hidden])
                msig = mask * sig
                edge = msig * proj[hidden:]
                msig_ref[side, block] = msig
                slope_ref[side, block] = edge * (1.0 - sig)
                for s in range(GROUP):
                    flip_ref[pl.ds(side * hidden * TILE + step * GROUP + s, hidden, stride=TILE), :] = edge[
                        :, s * lanes : (s + 1) * lanes
                    ]
            return carry

        lax.fori_loop(0, groups, project, 0)
        if chunk == 0:
            pl.semaphore_wait(barrier, peers - 1)

        def edge_block(owner):
            size = own_h * TILE
            return jnp.concatenate(
                [
                    flip_ref[pl.ds(pl.multiple_of(side * hidden * TILE + owner * size, size), size), :]
                    .reshape(own_h, TILE, lanes)
                    .astype(bf16)
                    for side in range(2)
                ],
                axis=0,
            )

        start_all(0, chunk, send_e, recv_e, edge_block)

    def assemble(recv, index, out_ref, h):
        for r in range(rows_n):
            for chunk in range(chunks):
                blocks = [recv[chunk, r * chs_n + c, index] for c in range(chs_n)]
                for ip in range(2):
                    row = r * rows + ip * half + chunk * TILE
                    out_ref[h, row : row + TILE, :] = jnp.concatenate(
                        [b[:, ip * cols : (ip + 1) * cols] for b in blocks], axis=1
                    )

    def scatter(values, send, chunk, index):
        for r in range(rows_n):
            for c in range(chs_n):
                part = values[r * rows : (r + 1) * rows, c * cols : (c + 1) * cols]
                send[chunk, r * chs_n + c, index] = jnp.concatenate([part[:half], part[half:]], axis=1)

    for chunk in range(chunks):
        wait_all(0, chunk, send_e, recv_e, None)
    for chunk in range(2):

        def multiply(step, carry):
            h = chunk * part_h + step
            assemble(recv_e, h, left_ref, h)
            assemble(recv_e, own_h + h, right_ref, h)
            tri = dot(left_ref[h], right_ref[h], (1, 1)).astype(bf16)
            scatter(tri, send_t, chunk, step)
            return carry

        lax.fori_loop(0, part_h, multiply, 0)
        start_all(1, chunk, send_t, recv_t, None)

    for chunk in range(2):

        def widen(origin):
            size = part_h * half
            row = pl.multiple_of((origin * 2 + chunk) * size, size)
            tri_ref[pl.ds(row, size), :] = recv_t[chunk, origin].reshape(size, lanes).astype(f32)

        wait_all(1, chunk, send_t, recv_t, widen)

    for chunk in range(chunks):

        def outward(step, carry):
            first = chunk * TILE + step * GROUP
            block = chunk * groups + step
            at = pl.ds(pl.multiple_of(block * wide, wide), wide)
            tri = jnp.concatenate(
                [tri_ref[pl.ds(first + s, hidden, stride=half), :] for s in range(GROUP)], axis=1
            )
            centered = tri - jnp.mean(tri, axis=0, keepdims=True)
            inv = lax.rsqrt(jnp.mean(centered * centered, axis=0, keepdims=True) + epsilon)
            hat = centered * inv
            gain = gout_ref[...]
            proj_out = dot((hat * gain).astype(bf16), ow_ref[...], (0, 0))
            gate = gate_ref[at, :]
            put_pairs(update_ref, first, (gate * proj_out).astype(bf16))
            cot_gate = pairs_of(cot_ref, first).astype(f32) * gate
            dgate_ref[at, :] = (cot_gate * proj_out * (1.0 - gate)).astype(bf16)
            d_hat = dot(ow_ref[...], cot_gate.astype(bf16), (1, 1)) * gain
            mean_a = jnp.mean(d_hat, axis=0, keepdims=True)
            mean_b = jnp.mean(d_hat * hat, axis=0, keepdims=True)
            d_tri = inv * (d_hat - mean_a - hat * mean_b)
            for s in range(GROUP):
                flip_ref[pl.ds(step * GROUP + s, hidden, stride=TILE), :] = d_tri[
                    :, s * lanes : (s + 1) * lanes
                ]
            return carry

        lax.fori_loop(0, groups, outward, 0)

        def d_tri_block(owner):
            size = own_h * TILE
            return (
                flip_ref[pl.ds(pl.multiple_of(owner * size, size), size), :]
                .reshape(own_h, TILE, lanes)
                .astype(bf16)
            )

        start_all(2, chunk, send_d, recv_d, d_tri_block)

    for chunk in range(chunks):
        wait_all(2, chunk, send_d, recv_d, None)
    for chunk in range(2):

        def multiply_back(step, carry):
            h = chunk * part_h + step
            assemble(recv_d, h, d_full_ref, 0)
            d_full = d_full_ref[0]
            scatter(dot(d_full, right_ref[h], (1, 0)).astype(bf16), send_g, chunk, step)
            scatter(dot(d_full, left_ref[h], (0, 0)).astype(bf16), send_g, chunk, part_h + step)
            return carry

        lax.fori_loop(0, part_h, multiply_back, 0)
        start_all(3, chunk, send_g, recv_g, None)

    for chunk in range(2):

        def widen_back(origin):
            size = part_h * half
            for side in range(2):
                row = pl.multiple_of(side * hidden * half + (origin * 2 + chunk) * size, size)
                back_ref[pl.ds(row, size), :] = (
                    recv_g[chunk, origin, side * part_h : (side + 1) * part_h].reshape(size, lanes).astype(f32)
                )

        wait_all(3, chunk, send_g, recv_g, widen_back)

    def inward(block, carry):
        first = block * GROUP
        at = pl.ds(pl.multiple_of(block * wide, wide), wide)
        d_normed = dot(dgate_ref[at, :], gw_ref[...], (1, 1))
        for side in range(2):
            d_edge = jnp.concatenate(
                [
                    back_ref[pl.ds(side * hidden * half + first + s, hidden, stride=half), :]
                    for s in range(GROUP)
                ],
                axis=1,
            )
            d_proj = jnp.concatenate(
                [
                    (d_edge * slope_ref[side, block]).astype(bf16),
                    (d_edge * msig_ref[side, block]).astype(bf16),
                ],
                axis=0,
            )
            d_normed = d_normed + dot(d_proj, wt_ref[pl.ds(2 * side * hidden, 2 * hidden), :], (0, 0))
        hat = hat_ref[at, :]
        d_hat = d_normed * gin_ref[...]
        mean_a = jnp.mean(d_hat, axis=-1, keepdims=True)
        mean_b = jnp.mean(d_hat * hat, axis=-1, keepdims=True)
        grad = inv_ref[at, :] * (d_hat - mean_a - hat * mean_b)
        put_pairs(grad_ref, first, grad.astype(bf16))
        return carry

    lax.fori_loop(0, half // GROUP, inward, 0)

    for chunk in range(chunks):
        wait_sends(0, chunk, send_e, recv_e)
        wait_sends(2, chunk, send_d, recv_d)
    for chunk in range(2):
        wait_sends(1, chunk, send_t, recv_t)
        wait_sends(3, chunk, send_g, recv_g)


def fused_device(
    rows_n, chs_n,
    pair_tensor, cotangent, residue_mask, in_gain, edge_weight, gate_weight, out_gain, out_weight,
):
    rows, cols, chans = pair_tensor.shape
    hidden = out_weight.shape[0]
    peers = rows_n * chs_n
    own_h = hidden // peers
    half, lanes, total = rows // 2, 2 * cols, rows * cols
    chunks = half // TILE
    side = rows_n * rows
    blocks = half // GROUP
    wide = GROUP * lanes
    live = residue_mask.astype(jnp.float32)
    live_rows = lax.dynamic_slice_in_dim(live, lax.axis_index("row") * rows, rows)
    live_cols = lax.dynamic_slice_in_dim(live, lax.axis_index("ch") * cols, cols)
    mask = live_rows.reshape(2, half).T[:, :, None] * live_cols[None, None, :]
    f32, bf16 = jnp.float32, jnp.bfloat16
    vm = pltpu.VMEM
    scratch = [
        vm((total, chans), f32),
        vm((total, chans), f32),
        vm((total, chans), f32),
        vm((total, chans), bf16),
        vm((2, blocks, hidden, wide), f32),
        vm((2, blocks, hidden, wide), f32),
        vm((2 * hidden * TILE, lanes), f32),
        vm((hidden * half, lanes), f32),
        vm((2 * hidden * half, lanes), f32),
        vm((own_h, side, side), bf16),
        vm((own_h, side, side), bf16),
        vm((1, side, side), bf16),
    ]
    for blocks_of in (
        (chunks, peers, 2 * own_h, TILE, lanes),
        (2, peers, own_h // 2, half, lanes),
        (chunks, peers, own_h, TILE, lanes),
        (2, peers, own_h, half, lanes),
    ):
        scratch += [vm(blocks_of, bf16), vm(blocks_of, bf16)]
    most = max(chunks, 2)
    scratch += [pltpu.SemaphoreType.DMA((4, most, peers)), pltpu.SemaphoreType.DMA((4, most, peers))]
    whole = pl.BlockSpec(memory_space=pltpu.VMEM)
    out = jax.ShapeDtypeStruct((rows, cols, chans), bf16)
    return pl.pallas_call(
        functools.partial(fused_kernel, rows_n, chs_n),
        out_shape=(out, out),
        in_specs=[whole] * 8,
        out_specs=(whole, whole),
        scratch_shapes=scratch,
        compiler_params=pltpu.CompilerParams(
            collective_id=0, has_side_effects=True, vmem_limit_bytes=56 * 1024 * 1024
        ),
    )(
        pair_tensor,
        cotangent,
        mask.reshape(half, lanes),
        in_gain.reshape(1, chans),
        edge_weight.transpose(0, 2, 1).reshape(4 * hidden, chans),
        gate_weight,
        out_gain.reshape(hidden, 1),
        out_weight,
    )


def solution(mesh):
    in_specs = (
        P(("grp", "row"), "ch", None),
        P(("grp", "row"), "ch", None),
        P("grp"),
        P(),
        P(),
        P(),
        P(),
        P(),
    )
    out_specs = (P(("grp", "row"), "ch", None), P(("grp", "row"), "ch", None))
    rows_n, chs_n = mesh.shape["row"], mesh.shape["ch"]
    body = per_device
    if 128 % (rows_n * chs_n) == 0 and (128 // (rows_n * chs_n)) % 2 == 0:
        body = functools.partial(fused_device, rows_n, chs_n)
    return jax.shard_map(
        body, mesh=mesh, in_specs=in_specs, out_specs=out_specs, check_vma=False
    )
```

```python
import functools

import jax
import jax.numpy as jnp
from jax import lax
from jax.experimental import pallas as pl
from jax.experimental.pallas import tpu as pltpu
from jax.sharding import PartitionSpec as P

epsilon = 1e-05


def normalize(values, axis):
    mean_val = jnp.mean(values, axis=axis, keepdims=True)
    centered = values - mean_val
    variance = jnp.mean(centered * centered, axis=axis, keepdims=True)
    inv_scale = lax.rsqrt(variance + epsilon)
    return (centered * inv_scale, inv_scale)


def layer_back(d_hat, hat, inv_scale, axis):
    first = jnp.mean(d_hat, axis=axis, keepdims=True)
    second = jnp.mean(d_hat * hat, axis=axis, keepdims=True)
    return inv_scale * (d_hat - first - hat * second)


def per_device(
    pair_tensor, cotangent, residue_mask, in_gain, edge_weight, gate_weight, out_gain, out_weight
):
    row_count = pair_tensor.shape[0]
    col_count = pair_tensor.shape[1]
    row_start = lax.axis_index("row") * row_count
    col_start = lax.axis_index("ch") * col_count
    live = residue_mask.astype(jnp.float32)
    live_rows = lax.dynamic_slice_in_dim(live, row_start, row_count)
    live_cols = lax.dynamic_slice_in_dim(live, col_start, col_count)
    pair_mask = live_rows[:, None] * live_cols[None, :]
    z_hat, inv_in = normalize(pair_tensor.astype(jnp.float32), -1)
    normed = (z_hat * in_gain).astype(jnp.bfloat16)
    proj = jnp.einsum("rjc,tch->thrj", normed, edge_weight, preferred_element_type=jnp.float32)
    shape_four = proj.shape
    proj_pairs = proj.reshape(2, 2, shape_four[1], row_count, col_count)
    edge_sig = jax.nn.sigmoid(proj_pairs[:, 0])
    edge_val = proj_pairs[:, 1]
    edges = (pair_mask * edge_sig * edge_val).astype(jnp.bfloat16)
    edge_chan = lax.all_to_all(edges, "ch", split_axis=1, concat_axis=3, tiled=True)
    left_c = edge_chan[0]
    right_c = edge_chan[1]
    shard_piece = lax.all_gather(right_c, "row", axis=1, tiled=True)
    block = jnp.einsum("hik,hjk->hij", left_c, shard_piece, preferred_element_type=jnp.float32)
    kept = shard_piece
    tri_full, kept = (block, kept)
    tri = tri_full.astype(jnp.bfloat16)
    tri_home = lax.all_to_all(tri, "ch", split_axis=2, concat_axis=0, tiled=True)
    t_hat, inv_tri = normalize(tri_home.astype(jnp.float32), 0)
    normed_tri = (t_hat * out_gain[:, None, None]).astype(jnp.bfloat16)
    proj_out = jnp.einsum("hrj,hc->rjc", normed_tri, out_weight, preferred_element_type=jnp.float32)
    gate = jax.nn.sigmoid(
        jnp.einsum("rjc,cd->rjd", normed, gate_weight, preferred_element_type=jnp.float32)
    )
    pair_update = (gate * proj_out).astype(jnp.bfloat16)
    grad_in = cotangent.astype(jnp.float32)
    d_out = (grad_in * gate).astype(jnp.bfloat16)
    d_gate = (grad_in * proj_out * gate * (1.0 - gate)).astype(jnp.bfloat16)
    d_ntri = jnp.einsum("rjc,hc->hrj", d_out, out_weight, preferred_element_type=jnp.float32)
    d_tri = layer_back(d_ntri * out_gain[:, None, None], t_hat, inv_tri, 0).astype(jnp.bfloat16)
    d_tri_c = lax.all_to_all(d_tri, "ch", split_axis=0, concat_axis=2, tiled=True)
    d_tri_t = lax.all_to_all(d_tri_c, "row", split_axis=2, concat_axis=1, tiled=True)
    d_left = jnp.einsum("hij,hjk->hik", d_tri_c, kept, preferred_element_type=jnp.float32)
    d_right = jnp.einsum(
        "hij,hik->hjk",
        d_tri_t,
        lax.all_gather(left_c, "row", axis=1, tiled=True),
        preferred_element_type=jnp.float32,
    )
    edge_grads = jnp.stack([d_left, d_right]).astype(jnp.bfloat16)
    grads_home = lax.all_to_all(edge_grads, "ch", split_axis=3, concat_axis=1, tiled=True)
    d_masked = grads_home.astype(jnp.float32) * pair_mask
    d_gates = d_masked * edge_val * edge_sig * (1.0 - edge_sig)
    d_values = d_masked * edge_sig
    d_proj = jnp.stack([d_gates, d_values], axis=1).reshape(shape_four).astype(jnp.bfloat16)
    d_normed = jnp.einsum("thrj,tch->rjc", d_proj, edge_weight, preferred_element_type=jnp.float32)
    d_normed = d_normed + jnp.einsum(
        "rjd,cd->rjc", d_gate, gate_weight, preferred_element_type=jnp.float32
    )
    grad_pair = layer_back(d_normed * in_gain, z_hat, inv_in, -1).astype(jnp.bfloat16)
    return (pair_update, grad_pair)


GROUP = 4
CHUNKS = 4


def dot(a, b, dims):
    return lax.dot_general(a, b, ((dims[:1], dims[1:]), ((), ())), preferred_element_type=jnp.float32)


def fused_kernel(
    rows_n, chs_n,
    x_ref, cot_ref, mask_ref, gin_ref, wt_ref, gw_ref, gout_ref, ow_ref,
    update_ref, grad_ref,
    hat_ref, inv_ref, gate_ref, normed_ref, dgate_ref, slope_ref, msig_ref,
    flip_ref, tri_ref, back_ref, left_ref, right_ref, d_full_ref, own_ref,
    send_e, recv_e, send_p, recv_p, send_t, recv_t, send_d, recv_d, send_g, recv_g,
    send_sem, recv_sem,
):
    f32, bf16 = jnp.float32, jnp.bfloat16
    zs = chs_n // 2
    peers = rows_n * zs
    rows, cols, chans = x_ref.shape
    half = rows // 2
    lanes = 2 * cols
    hidden = ow_ref.shape[0]
    own_h = hidden // peers
    part_h = own_h // CHUNKS
    chunk_h = hidden // CHUNKS
    size = part_h * half
    wide = GROUP * lanes
    groups = half // GROUP
    my_row, my_ch = lax.axis_index("row"), lax.axis_index("ch")
    my_side = my_ch // zs
    me = my_row * zs + lax.rem(my_ch, zs)

    def device(flat, side):
        return {"row": flat // zs, "ch": side * zs + lax.rem(flat, zs)}

    def ahead(offset):
        return lax.rem(me + offset, peers)

    def behind(offset):
        return lax.rem(me - offset + peers, peers)

    def make_copy(phase, chunk, index, source, landing, target, side):
        return pltpu.make_async_remote_copy(
            src_ref=source,
            dst_ref=landing,
            send_sem=send_sem.at[phase, chunk, index],
            recv_sem=recv_sem.at[phase, chunk, index],
            device_id=device(target, side),
            device_id_type=pl.DeviceIdType.MESH,
        )

    def near(phase, chunk, offset, send, recv, slot):
        target = ahead(offset)
        return make_copy(
            phase, chunk, offset, send.at[chunk, target], recv.at[chunk, slot], target, my_side
        )

    def start_near(phase, chunk, send, recv, fill):
        def step(offset, carry):
            if fill is not None:
                send[chunk, ahead(offset)] = fill(ahead(offset))
            near(phase, chunk, offset, send, recv, me).start()
            return carry

        lax.fori_loop(1, peers, step, 0)
        recv[chunk, me] = send[chunk, me] if fill is None else fill(me)

    def wait_near(phase, chunk, send, recv, use):
        if use is not None:
            use(me)

        def step(offset, carry):
            near(phase, chunk, offset, send, recv, behind(offset)).wait_recv()
            if use is not None:
                use(behind(offset))
            return carry

        lax.fori_loop(1, peers, step, 0)

    def across(chunk):
        return make_copy(1, chunk, 0, send_p.at[chunk], recv_p.at[chunk], me, 1 - my_side)

    def spread_near(chunk, offset, slot):
        target = ahead(offset)
        return make_copy(
            3, chunk, offset, send_d.at[chunk, target], recv_d.at[chunk, my_side * peers + slot], target, my_side
        )

    def spread_far(chunk, offset, side, slot):
        target = ahead(offset)
        return make_copy(
            3, chunk, peers + offset, send_d.at[chunk, target], recv_d.at[chunk, side * peers + slot],
            target, 1 - my_side,
        )

    def pairs_of(ref, first):
        low = ref[pl.ds(first, GROUP)]
        high = ref[pl.ds(first + half, GROUP)]
        return jnp.concatenate([low, high], axis=1).reshape(wide, chans)

    def put_pairs(ref, first, values):
        values = values.reshape(GROUP, lanes, chans)
        ref[pl.ds(first, GROUP)] = values[:, :cols]
        ref[pl.ds(first + half, GROUP)] = values[:, cols:]

    def pair_rows(block):
        return pl.ds(pl.multiple_of(block * wide, wide), wide)

    barrier = pltpu.get_barrier_semaphore()

    def greet(offset, carry):
        flat = lax.rem(my_side * peers + me + offset, 2 * peers)
        pl.semaphore_signal(
            barrier, inc=1, device_id=device(lax.rem(flat, peers), flat // peers),
            device_id_type=pl.DeviceIdType.MESH,
        )
        return carry

    lax.fori_loop(1, 2 * peers, greet, 0)

    def prepare(block, carry):
        at = pair_rows(block)
        x = pairs_of(x_ref, block * GROUP).astype(f32)
        centered = x - jnp.mean(x, axis=-1, keepdims=True)
        inv = lax.rsqrt(jnp.mean(centered * centered, axis=-1, keepdims=True) + epsilon)
        hat = centered * inv
        hat_ref[at, :] = hat
        inv_ref[at, :] = jnp.broadcast_to(inv, (wide, chans))
        normed_ref[at, :] = (hat * gin_ref[...]).astype(bf16)
        return carry

    lax.fori_loop(0, groups, prepare, 0)

    for chunk in range(CHUNKS):
        weights = jnp.concatenate(
            [wt_ref[t * hidden + chunk * chunk_h : t * hidden + (chunk + 1) * chunk_h, :] for t in range(4)],
            axis=0,
        )

        def project(block, carry):
            first = block * GROUP
            mask = jnp.concatenate([mask_ref[pl.ds(first + s, 1), :] for s in range(GROUP)], axis=1)
            proj = dot(weights, normed_ref[pair_rows(block), :], (1, 1))
            for side in range(2):
                base = 2 * side * chunk_h
                sig = jax.nn.sigmoid(proj[base : base + chunk_h])
                msig = mask * sig
                edge = msig * proj[base + chunk_h : base + 2 * chunk_h]
                kept = pl.ds(chunk * chunk_h, chunk_h)
                msig_ref[side, block, kept, :] = msig
                slope_ref[side, block, kept, :] = edge * (1.0 - sig)
                for s in range(GROUP):
                    flip_ref[pl.ds(side * chunk_h * half + first + s, chunk_h, stride=half), :] = edge[
                        :, s * lanes : (s + 1) * lanes
                    ]
            return carry

        lax.fori_loop(0, groups, project, 0)
        if chunk == 0:
            pl.semaphore_wait(barrier, 2 * peers - 1)

        def edge_block(owner):
            return jnp.concatenate(
                [
                    flip_ref[pl.ds(pl.multiple_of(side * chunk_h * half + owner * size, size), size), :]
                    .reshape(part_h, half, lanes)
                    .astype(bf16)
                    for side in range(2)
                ],
                axis=0,
            )

        start_near(0, chunk, send_e, recv_e, edge_block)

    def open_gate(block, carry):
        at = pair_rows(block)
        gate_ref[at, :] = jax.nn.sigmoid(dot(normed_ref[at, :], gw_ref[...], (1, 0)))
        return carry

    lax.fori_loop(0, groups, open_gate, 0)

    def assemble(blocks_of, out_ref, h):
        for r in range(rows_n):
            blocks = blocks_of(r)
            for ip in range(2):
                row = r * rows + ip * half
                out_ref[h, row : row + half, :] = jnp.concatenate(
                    [b[:, ip * cols : (ip + 1) * cols] for b in blocks], axis=1
                )

    def scatter(values, send, chunk, index):
        for r in range(rows_n):
            for c in range(zs):
                part = values[r * rows : (r + 1) * rows, c * cols : (c + 1) * cols]
                send[chunk, r * zs + c, index] = jnp.concatenate([part[:half], part[half:]], axis=1)

    reach = zs * cols
    for chunk in range(CHUNKS):
        wait_near(0, chunk, send_e, recv_e, None)

        def multiply(step, carry):
            h = chunk * part_h + step
            for side, out_ref in ((0, left_ref), (1, right_ref)):
                assemble(
                    lambda r: [recv_e[chunk, r * zs + c, side * part_h + step] for c in range(zs)], out_ref, h
                )
            mine = right_ref[h, pl.ds(pl.multiple_of(my_side * reach, reach), reach), :]
            other = right_ref[h, pl.ds(pl.multiple_of((1 - my_side) * reach, reach), reach), :]
            send_p[chunk, step] = dot(left_ref[h], other, (1, 1)).astype(bf16)
            own_ref[h] = dot(left_ref[h], mine, (1, 1))
            return carry

        lax.fori_loop(0, part_h, multiply, 0)
        across(chunk).start()

    for chunk in range(CHUNKS):
        across(chunk).wait_recv()

        def total(step, carry):
            tri = own_ref[chunk * part_h + step] + recv_p[chunk, step].astype(f32)
            scatter(tri.astype(bf16), send_t, chunk, step)
            return carry

        lax.fori_loop(0, part_h, total, 0)
        start_near(2, chunk, send_t, recv_t, None)

    for chunk in range(CHUNKS):

        def widen(origin):
            row = pl.multiple_of((origin * CHUNKS + chunk) * size, size)
            tri_ref[pl.ds(row, size), :] = recv_t[chunk, origin].reshape(size, lanes).astype(f32)

        wait_near(2, chunk, send_t, recv_t, widen)

    def outward(block, carry):
        first = block * GROUP
        at = pair_rows(block)
        tri = jnp.concatenate(
            [tri_ref[pl.ds(first + s, hidden, stride=half), :] for s in range(GROUP)], axis=1
        )
        centered = tri - jnp.mean(tri, axis=0, keepdims=True)
        inv = lax.rsqrt(jnp.mean(centered * centered, axis=0, keepdims=True) + epsilon)
        hat = centered * inv
        gain = gout_ref[...]
        proj_out = dot((hat * gain).astype(bf16), ow_ref[...], (0, 0))
        gate = gate_ref[at, :]
        put_pairs(update_ref, first, (gate * proj_out).astype(bf16))
        cot_gate = pairs_of(cot_ref, first).astype(f32) * gate
        dgate_ref[at, :] = (cot_gate * proj_out * (1.0 - gate)).astype(bf16)
        d_hat = dot(ow_ref[...], cot_gate.astype(bf16), (1, 1)) * gain
        mean_a = jnp.mean(d_hat, axis=0, keepdims=True)
        mean_b = jnp.mean(d_hat * hat, axis=0, keepdims=True)
        d_tri = inv * (d_hat - mean_a - hat * mean_b)
        for s in range(GROUP):
            tri_ref[pl.ds(first + s, hidden, stride=half), :] = d_tri[:, s * lanes : (s + 1) * lanes]
        return carry

    lax.fori_loop(0, groups, outward, 0)

    def d_tri_block(chunk, owner):
        row = pl.multiple_of((owner * CHUNKS + chunk) * size, size)
        return tri_ref[pl.ds(row, size), :].reshape(part_h, half, lanes).astype(bf16)

    for chunk in range(CHUNKS):
        mine = d_tri_block(chunk, me)
        send_d[chunk, me] = mine
        recv_d[chunk, my_side * peers + me] = mine
        spread_far(chunk, 0, my_side, me).start()

        def spread(offset, carry):
            send_d[chunk, ahead(offset)] = d_tri_block(chunk, ahead(offset))
            spread_far(chunk, offset, my_side, me).start()
            spread_near(chunk, offset, me).start()
            return carry

        lax.fori_loop(1, peers, spread, 0)

    for chunk in range(CHUNKS):
        spread_far(chunk, 0, 1 - my_side, me).wait_recv()

        def gathered(offset, carry):
            spread_far(chunk, offset, 1 - my_side, behind(offset)).wait_recv()
            spread_near(chunk, offset, behind(offset)).wait_recv()
            return carry

        lax.fori_loop(1, peers, gathered, 0)

        def multiply_back(step, carry):
            h = chunk * part_h + step
            assemble(
                lambda r: [recv_d[chunk, (c // zs) * peers + r * zs + c % zs, step] for c in range(chs_n)],
                d_full_ref,
                0,
            )
            d_full = d_full_ref[0]
            scatter(dot(d_full, right_ref[h], (1, 0)).astype(bf16), send_g, chunk, step)
            scatter(dot(d_full, left_ref[h], (0, 0)).astype(bf16), send_g, chunk, part_h + step)
            return carry

        lax.fori_loop(0, part_h, multiply_back, 0)
        start_near(4, chunk, send_g, recv_g, None)

    for chunk in range(CHUNKS):

        def widen_back(origin):
            for side in range(2):
                row = pl.multiple_of(((side * CHUNKS + chunk) * peers + origin) * size, size)
                back_ref[pl.ds(row, size), :] = (
                    recv_g[chunk, origin, side * part_h : (side + 1) * part_h].reshape(size, lanes).astype(f32)
                )

        wait_near(4, chunk, send_g, recv_g, widen_back)
    def inward(block, carry):
        first = block * GROUP
        at = pair_rows(block)
        d_normed = dot(dgate_ref[at, :], gw_ref[...], (1, 1))
        for side in range(2):
            d_edge = jnp.concatenate(
                [
                    back_ref[pl.ds(side * hidden * half + first + s, hidden, stride=half), :]
                    for s in range(GROUP)
                ],
                axis=1,
            )
            d_proj = jnp.concatenate(
                [
                    (d_edge * slope_ref[side, block]).astype(bf16),
                    (d_edge * msig_ref[side, block]).astype(bf16),
                ],
                axis=0,
            )
            d_normed = d_normed + dot(d_proj, wt_ref[pl.ds(2 * side * hidden, 2 * hidden), :], (0, 0))
        hat = hat_ref[at, :]
        d_hat = d_normed * gin_ref[...]
        mean_a = jnp.mean(d_hat, axis=-1, keepdims=True)
        mean_b = jnp.mean(d_hat * hat, axis=-1, keepdims=True)
        grad = inv_ref[at, :] * (d_hat - mean_a - hat * mean_b)
        put_pairs(grad_ref, first, grad.astype(bf16))
        return carry

    lax.fori_loop(0, groups, inward, 0)

    for chunk in range(CHUNKS):
        across(chunk).wait_send()
        spread_far(chunk, 0, my_side, me).wait_send()

        def finish(offset, carry):
            near(0, chunk, offset, send_e, recv_e, me).wait_send()
            near(2, chunk, offset, send_t, recv_t, me).wait_send()
            near(4, chunk, offset, send_g, recv_g, me).wait_send()
            spread_near(chunk, offset, me).wait_send()
            spread_far(chunk, offset, my_side, me).wait_send()
            return carry

        lax.fori_loop(1, peers, finish, 0)


def fused_device(
    rows_n, chs_n,
    pair_tensor, cotangent, residue_mask, in_gain, edge_weight, gate_weight, out_gain, out_weight,
):
    rows, cols, chans = pair_tensor.shape
    hidden = out_weight.shape[0]
    peers = rows_n * (chs_n // 2)
    own_h = hidden // peers
    half, lanes, total = rows // 2, 2 * cols, rows * cols
    side = rows_n * rows
    blocks = half // GROUP
    wide = GROUP * lanes
    live = residue_mask.astype(jnp.float32)
    live_rows = lax.dynamic_slice_in_dim(live, lax.axis_index("row") * rows, rows)
    live_cols = lax.dynamic_slice_in_dim(live, lax.axis_index("ch") * cols, cols)
    mask = live_rows.reshape(2, half).T[:, :, None] * live_cols[None, None, :]
    f32, bf16 = jnp.float32, jnp.bfloat16
    vm = pltpu.VMEM
    zs = chs_n // 2
    reach = zs * cols
    part_h = own_h // CHUNKS
    scratch = [
        vm((total, chans), f32),
        vm((total, chans), f32),
        vm((total, chans), f32),
        vm((total, chans), bf16),
        vm((total, chans), bf16),
        vm((2, blocks, hidden, wide), f32),
        vm((2, blocks, hidden, wide), f32),
        vm((2 * (hidden // CHUNKS) * half, lanes), f32),
        vm((hidden * half, lanes), f32),
        vm((2 * hidden * half, lanes), f32),
        vm((own_h, side, reach), bf16),
        vm((own_h, side, reach), bf16),
        vm((1, side, side), bf16),
        vm((own_h, side, reach), f32),
    ]
    edge_slots = vm((CHUNKS, peers, 2 * part_h, half, lanes), bf16)
    part_slots = vm((CHUNKS, part_h, side, reach), bf16)
    tri_slots = vm((CHUNKS, peers, part_h, half, lanes), bf16)
    both_slots = vm((CHUNKS, 2 * peers, part_h, half, lanes), bf16)
    scratch += [edge_slots, edge_slots, part_slots, part_slots, tri_slots, tri_slots]
    scratch += [tri_slots, both_slots, edge_slots, edge_slots]
    sems = pltpu.SemaphoreType.DMA((5, CHUNKS, 2 * peers))
    scratch += [sems, sems]
    whole = pl.BlockSpec(memory_space=pltpu.VMEM)
    out = jax.ShapeDtypeStruct((rows, cols, chans), bf16)
    return pl.pallas_call(
        functools.partial(fused_kernel, rows_n, chs_n),
        out_shape=(out, out),
        in_specs=[whole] * 8,
        out_specs=(whole, whole),
        scratch_shapes=scratch,
        compiler_params=pltpu.CompilerParams(
            collective_id=0, has_side_effects=True, vmem_limit_bytes=56 * 1024 * 1024
        ),
    )(
        pair_tensor,
        cotangent,
        mask.reshape(half, lanes),
        in_gain.reshape(1, chans),
        edge_weight.reshape(4, chans, peers, CHUNKS, part_h)
        .transpose(0, 3, 2, 4, 1)
        .reshape(4 * hidden, chans),
        gate_weight,
        out_gain.reshape(hidden, 1),
        out_weight,
    )


def solution(mesh):
    in_specs = (
        P(("grp", "row"), "ch", None),
        P(("grp", "row"), "ch", None),
        P("grp"),
        P(),
        P(),
        P(),
        P(),
        P(),
    )
    out_specs = (P(("grp", "row"), "ch", None), P(("grp", "row"), "ch", None))
    rows_n, chs_n = mesh.shape["row"], mesh.shape["ch"]
    body = per_device
    owners = rows_n * chs_n // 2
    if chs_n % 2 == 0 and 128 % (owners * CHUNKS) == 0:
        body = functools.partial(fused_device, rows_n, chs_n)
    return jax.shard_map(
        body, mesh=mesh, in_specs=in_specs, out_specs=out_specs, check_vma=False
    )
```

```python
import functools

import jax
import jax.numpy as jnp
from jax import lax
from jax.experimental import pallas as pl
from jax.experimental.pallas import tpu as pltpu
from jax.sharding import PartitionSpec as P

epsilon = 1e-05


def normalize(values, axis):
    mean_val = jnp.mean(values, axis=axis, keepdims=True)
    centered = values - mean_val
    variance = jnp.mean(centered * centered, axis=axis, keepdims=True)
    inv_scale = lax.rsqrt(variance + epsilon)
    return (centered * inv_scale, inv_scale)


def layer_back(d_hat, hat, inv_scale, axis):
    first = jnp.mean(d_hat, axis=axis, keepdims=True)
    second = jnp.mean(d_hat * hat, axis=axis, keepdims=True)
    return inv_scale * (d_hat - first - hat * second)


def per_device(
    pair_tensor, cotangent, residue_mask, in_gain, edge_weight, gate_weight, out_gain, out_weight
):
    row_count = pair_tensor.shape[0]
    col_count = pair_tensor.shape[1]
    row_start = lax.axis_index("row") * row_count
    col_start = lax.axis_index("ch") * col_count
    live = residue_mask.astype(jnp.float32)
    live_rows = lax.dynamic_slice_in_dim(live, row_start, row_count)
    live_cols = lax.dynamic_slice_in_dim(live, col_start, col_count)
    pair_mask = live_rows[:, None] * live_cols[None, :]
    z_hat, inv_in = normalize(pair_tensor.astype(jnp.float32), -1)
    normed = (z_hat * in_gain).astype(jnp.bfloat16)
    proj = jnp.einsum("rjc,tch->thrj", normed, edge_weight, preferred_element_type=jnp.float32)
    shape_four = proj.shape
    proj_pairs = proj.reshape(2, 2, shape_four[1], row_count, col_count)
    edge_sig = jax.nn.sigmoid(proj_pairs[:, 0])
    edge_val = proj_pairs[:, 1]
    edges = (pair_mask * edge_sig * edge_val).astype(jnp.bfloat16)
    edge_chan = lax.all_to_all(edges, "ch", split_axis=1, concat_axis=3, tiled=True)
    left_c = edge_chan[0]
    right_c = edge_chan[1]
    shard_piece = lax.all_gather(right_c, "row", axis=1, tiled=True)
    block = jnp.einsum("hik,hjk->hij", left_c, shard_piece, preferred_element_type=jnp.float32)
    kept = shard_piece
    tri_full, kept = (block, kept)
    tri = tri_full.astype(jnp.bfloat16)
    tri_home = lax.all_to_all(tri, "ch", split_axis=2, concat_axis=0, tiled=True)
    t_hat, inv_tri = normalize(tri_home.astype(jnp.float32), 0)
    normed_tri = (t_hat * out_gain[:, None, None]).astype(jnp.bfloat16)
    proj_out = jnp.einsum("hrj,hc->rjc", normed_tri, out_weight, preferred_element_type=jnp.float32)
    gate = jax.nn.sigmoid(
        jnp.einsum("rjc,cd->rjd", normed, gate_weight, preferred_element_type=jnp.float32)
    )
    pair_update = (gate * proj_out).astype(jnp.bfloat16)
    grad_in = cotangent.astype(jnp.float32)
    d_out = (grad_in * gate).astype(jnp.bfloat16)
    d_gate = (grad_in * proj_out * gate * (1.0 - gate)).astype(jnp.bfloat16)
    d_ntri = jnp.einsum("rjc,hc->hrj", d_out, out_weight, preferred_element_type=jnp.float32)
    d_tri = layer_back(d_ntri * out_gain[:, None, None], t_hat, inv_tri, 0).astype(jnp.bfloat16)
    d_tri_c = lax.all_to_all(d_tri, "ch", split_axis=0, concat_axis=2, tiled=True)
    d_tri_t = lax.all_to_all(d_tri_c, "row", split_axis=2, concat_axis=1, tiled=True)
    d_left = jnp.einsum("hij,hjk->hik", d_tri_c, kept, preferred_element_type=jnp.float32)
    d_right = jnp.einsum(
        "hij,hik->hjk",
        d_tri_t,
        lax.all_gather(left_c, "row", axis=1, tiled=True),
        preferred_element_type=jnp.float32,
    )
    edge_grads = jnp.stack([d_left, d_right]).astype(jnp.bfloat16)
    grads_home = lax.all_to_all(edge_grads, "ch", split_axis=3, concat_axis=1, tiled=True)
    d_masked = grads_home.astype(jnp.float32) * pair_mask
    d_gates = d_masked * edge_val * edge_sig * (1.0 - edge_sig)
    d_values = d_masked * edge_sig
    d_proj = jnp.stack([d_gates, d_values], axis=1).reshape(shape_four).astype(jnp.bfloat16)
    d_normed = jnp.einsum("thrj,tch->rjc", d_proj, edge_weight, preferred_element_type=jnp.float32)
    d_normed = d_normed + jnp.einsum(
        "rjd,cd->rjc", d_gate, gate_weight, preferred_element_type=jnp.float32
    )
    grad_pair = layer_back(d_normed * in_gain, z_hat, inv_in, -1).astype(jnp.bfloat16)
    return (pair_update, grad_pair)


GROUP = 4
CHUNKS = 4


def dot(a, b, dims):
    return lax.dot_general(a, b, ((dims[:1], dims[1:]), ((), ())), preferred_element_type=jnp.float32)


def fused_kernel(
    rows_n, chs_n,
    x_ref, cot_ref, mask_ref, gin_ref, wt_ref, gw_ref, gout_ref, ow_ref,
    update_ref, grad_ref,
    hat_ref, inv_ref, gate_ref, normed_ref, slope_ref, msig_ref,
    flip_ref, tri_ref, back_ref, left_ref, right_ref, d_full_ref, own_ref, dhat_ref, ntri_ref,
    send_e, recv_e, send_p, recv_p, send_t, recv_t, send_d, recv_d, send_g, recv_g,
    send_sem, recv_sem,
):
    f32, bf16 = jnp.float32, jnp.bfloat16
    zs = chs_n // 2
    peers = rows_n * zs
    rows, cols, chans = x_ref.shape
    half = rows // 2
    lanes = 2 * cols
    hidden = ow_ref.shape[0]
    own_h = hidden // peers
    part_h = own_h // CHUNKS
    chunk_h = hidden // CHUNKS
    size = part_h * half
    wide = GROUP * lanes
    groups = half // GROUP
    my_row, my_ch = lax.axis_index("row"), lax.axis_index("ch")
    my_side = my_ch // zs
    me = my_row * zs + lax.rem(my_ch, zs)

    def device(flat, side):
        return {"row": flat // zs, "ch": side * zs + lax.rem(flat, zs)}

    def ahead(offset):
        return lax.rem(me + offset, peers)

    def behind(offset):
        return lax.rem(me - offset + peers, peers)

    def make_copy(phase, chunk, index, source, landing, target, side):
        return pltpu.make_async_remote_copy(
            src_ref=source,
            dst_ref=landing,
            send_sem=send_sem.at[phase, chunk, index],
            recv_sem=recv_sem.at[phase, chunk, index],
            device_id=device(target, side),
            device_id_type=pl.DeviceIdType.MESH,
        )

    def near(phase, chunk, offset, send, recv, slot):
        target = ahead(offset)
        return make_copy(
            phase, chunk, offset, send.at[chunk, target], recv.at[chunk, slot], target, my_side
        )

    def start_near(phase, chunk, send, recv, fill):
        def step(offset, carry):
            if fill is not None:
                send[chunk, ahead(offset)] = fill(ahead(offset))
            near(phase, chunk, offset, send, recv, me).start()
            return carry

        lax.fori_loop(1, peers, step, 0)
        recv[chunk, me] = send[chunk, me] if fill is None else fill(me)

    def wait_near(phase, chunk, send, recv, use):
        if use is not None:
            use(me)

        def step(offset, carry):
            near(phase, chunk, offset, send, recv, behind(offset)).wait_recv()
            if use is not None:
                use(behind(offset))
            return carry

        lax.fori_loop(1, peers, step, 0)

    def across(chunk):
        return make_copy(1, chunk, 0, send_p.at[chunk], recv_p.at[chunk], me, 1 - my_side)

    def spread_near(chunk, offset, slot):
        target = ahead(offset)
        return make_copy(
            3, chunk, offset, send_d.at[chunk, target], recv_d.at[chunk, my_side * peers + slot], target, my_side
        )

    def spread_far(chunk, offset, side, slot):
        target = ahead(offset)
        return make_copy(
            3, chunk, peers + offset, send_d.at[chunk, target], recv_d.at[chunk, side * peers + slot],
            target, 1 - my_side,
        )

    def pairs_of(ref, first):
        low = ref[pl.ds(first, GROUP)]
        high = ref[pl.ds(first + half, GROUP)]
        return jnp.concatenate([low, high], axis=1).reshape(wide, chans)

    def put_pairs(ref, first, values):
        values = values.reshape(GROUP, lanes, chans)
        ref[pl.ds(first, GROUP)] = values[:, :cols]
        ref[pl.ds(first + half, GROUP)] = values[:, cols:]

    def pair_rows(block):
        return pl.ds(pl.multiple_of(block * wide, wide), wide)

    barrier = pltpu.get_barrier_semaphore()

    def greet(offset, carry):
        flat = lax.rem(my_side * peers + me + offset, 2 * peers)
        pl.semaphore_signal(
            barrier, inc=1, device_id=device(lax.rem(flat, peers), flat // peers),
            device_id_type=pl.DeviceIdType.MESH,
        )
        return carry

    lax.fori_loop(1, 2 * peers, greet, 0)

    def prepare(block, carry):
        at = pair_rows(block)
        x = pairs_of(x_ref, block * GROUP).astype(f32)
        centered = x - jnp.mean(x, axis=-1, keepdims=True)
        inv = lax.rsqrt(jnp.mean(centered * centered, axis=-1, keepdims=True) + epsilon)
        hat = centered * inv
        hat_ref[at, :] = hat
        inv_ref[at, :] = jnp.broadcast_to(inv, (wide, chans))
        normed_ref[at, :] = (hat * gin_ref[...]).astype(bf16)
        return carry

    lax.fori_loop(0, groups, prepare, 0)

    def chunk_weights(chunk):
        return jnp.concatenate(
            [wt_ref[t * hidden + chunk * chunk_h : t * hidden + (chunk + 1) * chunk_h, :] for t in range(4)],
            axis=0,
        )

    for chunk in range(CHUNKS):
        weights = chunk_weights(chunk)

        def project(block, carry):
            first = block * GROUP
            mask = jnp.concatenate([mask_ref[pl.ds(first + s, 1), :] for s in range(GROUP)], axis=1)
            proj = dot(weights, normed_ref[pair_rows(block), :], (1, 1))
            for side in range(2):
                base = 2 * side * chunk_h
                sig = jax.nn.sigmoid(proj[base : base + chunk_h])
                msig = mask * sig
                edge = msig * proj[base + chunk_h : base + 2 * chunk_h]
                kept = pl.ds(chunk * chunk_h, chunk_h)
                msig_ref[side, block, kept, :] = msig
                slope_ref[side, block, kept, :] = edge * (1.0 - sig)
                for s in range(GROUP):
                    flip_ref[pl.ds(side * chunk_h * half + first + s, chunk_h, stride=half), :] = edge[
                        :, s * lanes : (s + 1) * lanes
                    ]
            return carry

        lax.fori_loop(0, groups, project, 0)
        if chunk == 0:
            pl.semaphore_wait(barrier, 2 * peers - 1)

        def edge_block(owner):
            return jnp.concatenate(
                [
                    flip_ref[pl.ds(pl.multiple_of(side * chunk_h * half + owner * size, size), size), :]
                    .reshape(part_h, half, lanes)
                    .astype(bf16)
                    for side in range(2)
                ],
                axis=0,
            )

        start_near(0, chunk, send_e, recv_e, edge_block)

    def open_gate(block, carry):
        at = pair_rows(block)
        gate = jax.nn.sigmoid(dot(normed_ref[at, :], gw_ref[...], (1, 0)))
        gate_ref[at, :] = gate
        d_out = (pairs_of(cot_ref, block * GROUP).astype(f32) * gate).astype(bf16)
        dhat_ref[block] = dot(ow_ref[...], d_out, (1, 1)) * gout_ref[...]
        return carry

    lax.fori_loop(0, groups, open_gate, 0)

    def assemble(blocks_of, out_ref, h):
        for r in range(rows_n):
            blocks = blocks_of(r)
            for ip in range(2):
                row = r * rows + ip * half
                out_ref[h, row : row + half, :] = jnp.concatenate(
                    [b[:, ip * cols : (ip + 1) * cols] for b in blocks], axis=1
                )

    def scatter(values, send, chunk, index):
        for r in range(rows_n):
            for c in range(zs):
                part = values[r * rows : (r + 1) * rows, c * cols : (c + 1) * cols]
                send[chunk, r * zs + c, index] = jnp.concatenate([part[:half], part[half:]], axis=1)

    reach = zs * cols
    for chunk in range(CHUNKS):
        wait_near(0, chunk, send_e, recv_e, None)

        def multiply(step, carry):
            h = chunk * part_h + step
            for side, out_ref in ((0, left_ref), (1, right_ref)):
                assemble(
                    lambda r: [recv_e[chunk, r * zs + c, side * part_h + step] for c in range(zs)], out_ref, h
                )
            mine = right_ref[h, pl.ds(pl.multiple_of(my_side * reach, reach), reach), :]
            other = right_ref[h, pl.ds(pl.multiple_of((1 - my_side) * reach, reach), reach), :]
            send_p[chunk, step] = dot(left_ref[h], other, (1, 1)).astype(bf16)
            own_ref[h] = dot(left_ref[h], mine, (1, 1))
            return carry

        lax.fori_loop(0, part_h, multiply, 0)
        across(chunk).start()

    for chunk in range(CHUNKS):
        across(chunk).wait_recv()

        def total(step, carry):
            tri = own_ref[chunk * part_h + step] + recv_p[chunk, step].astype(f32)
            scatter(tri.astype(bf16), send_t, chunk, step)
            return carry

        lax.fori_loop(0, part_h, total, 0)
        start_near(2, chunk, send_t, recv_t, None)

    for chunk in range(CHUNKS):

        def widen(origin):
            row = pl.multiple_of((origin * CHUNKS + chunk) * size, size)
            tri_ref[pl.ds(row, size), :] = recv_t[chunk, origin].reshape(size, lanes).astype(f32)

        wait_near(2, chunk, send_t, recv_t, widen)

    def outward(block, carry):
        first = block * GROUP
        tri = jnp.concatenate(
            [tri_ref[pl.ds(first + s, hidden, stride=half), :] for s in range(GROUP)], axis=1
        )
        centered = tri - jnp.mean(tri, axis=0, keepdims=True)
        inv = lax.rsqrt(jnp.mean(centered * centered, axis=0, keepdims=True) + epsilon)
        hat = centered * inv
        ntri_ref[block] = (hat * gout_ref[...]).astype(bf16)
        d_hat = dhat_ref[block]
        mean_a = jnp.mean(d_hat, axis=0, keepdims=True)
        mean_b = jnp.mean(d_hat * hat, axis=0, keepdims=True)
        d_tri = inv * (d_hat - mean_a - hat * mean_b)
        for s in range(GROUP):
            tri_ref[pl.ds(first + s, hidden, stride=half), :] = d_tri[:, s * lanes : (s + 1) * lanes]
        return carry

    lax.fori_loop(0, groups, outward, 0)

    def d_tri_block(chunk, owner):
        row = pl.multiple_of((owner * CHUNKS + chunk) * size, size)
        return tri_ref[pl.ds(row, size), :].reshape(part_h, half, lanes).astype(bf16)

    for chunk in range(CHUNKS):
        mine = d_tri_block(chunk, me)
        send_d[chunk, me] = mine
        recv_d[chunk, my_side * peers + me] = mine
        spread_far(chunk, 0, my_side, me).start()

        def spread(offset, carry):
            send_d[chunk, ahead(offset)] = d_tri_block(chunk, ahead(offset))
            spread_far(chunk, offset, my_side, me).start()
            spread_near(chunk, offset, me).start()
            return carry

        lax.fori_loop(1, peers, spread, 0)

    def update(block, carry):
        first = block * GROUP
        at = pair_rows(block)
        proj_out = dot(ntri_ref[block], ow_ref[...], (0, 0))
        gate = gate_ref[at, :]
        put_pairs(update_ref, first, (gate * proj_out).astype(bf16))
        d_gate = pairs_of(cot_ref, first).astype(f32) * proj_out * gate * (1.0 - gate)
        gate_ref[at, :] = dot(d_gate.astype(bf16), gw_ref[...], (1, 1))
        return carry

    lax.fori_loop(0, groups, update, 0)

    for chunk in range(CHUNKS):
        spread_far(chunk, 0, 1 - my_side, me).wait_recv()

        def gathered(offset, carry):
            spread_far(chunk, offset, 1 - my_side, behind(offset)).wait_recv()
            spread_near(chunk, offset, behind(offset)).wait_recv()
            return carry

        lax.fori_loop(1, peers, gathered, 0)

        def multiply_back(step, carry):
            h = chunk * part_h + step
            assemble(
                lambda r: [recv_d[chunk, (c // zs) * peers + r * zs + c % zs, step] for c in range(chs_n)],
                d_full_ref,
                0,
            )
            d_full = d_full_ref[0]
            scatter(dot(d_full, right_ref[h], (1, 0)).astype(bf16), send_g, chunk, step)
            scatter(dot(d_full, left_ref[h], (0, 0)).astype(bf16), send_g, chunk, part_h + step)
            return carry

        lax.fori_loop(0, part_h, multiply_back, 0)
        start_near(4, chunk, send_g, recv_g, None)

    for chunk in range(CHUNKS):

        def widen_back(origin):
            for side in range(2):
                row = pl.multiple_of(((side * CHUNKS + chunk) * peers + origin) * size, size)
                back_ref[pl.ds(row, size), :] = (
                    recv_g[chunk, origin, side * part_h : (side + 1) * part_h].reshape(size, lanes).astype(f32)
                )

        wait_near(4, chunk, send_g, recv_g, widen_back)
        weights = chunk_weights(chunk)

        def inward(block, carry):
            first = block * GROUP
            at = pair_rows(block)
            kept = pl.ds(chunk * chunk_h, chunk_h)
            parts = []
            for side in range(2):
                row = (side * CHUNKS + chunk) * chunk_h * half
                d_edge = jnp.concatenate(
                    [back_ref[pl.ds(row + first + s, chunk_h, stride=half), :] for s in range(GROUP)], axis=1
                )
                parts.append((d_edge * slope_ref[side, block, kept, :]).astype(bf16))
                parts.append((d_edge * msig_ref[side, block, kept, :]).astype(bf16))
            d_normed = gate_ref[at, :] + dot(jnp.concatenate(parts, axis=0), weights, (0, 0))
            if chunk < CHUNKS - 1:
                gate_ref[at, :] = d_normed
                return carry
            hat = hat_ref[at, :]
            d_hat = d_normed * gin_ref[...]
            mean_a = jnp.mean(d_hat, axis=-1, keepdims=True)
            mean_b = jnp.mean(d_hat * hat, axis=-1, keepdims=True)
            grad = inv_ref[at, :] * (d_hat - mean_a - hat * mean_b)
            put_pairs(grad_ref, first, grad.astype(bf16))
            return carry

        lax.fori_loop(0, groups, inward, 0)

    for chunk in range(CHUNKS):
        across(chunk).wait_send()
        spread_far(chunk, 0, my_side, me).wait_send()

        def finish(offset, carry):
            near(0, chunk, offset, send_e, recv_e, me).wait_send()
            near(2, chunk, offset, send_t, recv_t, me).wait_send()
            near(4, chunk, offset, send_g, recv_g, me).wait_send()
            spread_near(chunk, offset, me).wait_send()
            spread_far(chunk, offset, my_side, me).wait_send()
            return carry

        lax.fori_loop(1, peers, finish, 0)


def fused_device(
    rows_n, chs_n,
    pair_tensor, cotangent, residue_mask, in_gain, edge_weight, gate_weight, out_gain, out_weight,
):
    rows, cols, chans = pair_tensor.shape
    hidden = out_weight.shape[0]
    peers = rows_n * (chs_n // 2)
    own_h = hidden // peers
    half, lanes, total = rows // 2, 2 * cols, rows * cols
    side = rows_n * rows
    blocks = half // GROUP
    wide = GROUP * lanes
    live = residue_mask.astype(jnp.float32)
    live_rows = lax.dynamic_slice_in_dim(live, lax.axis_index("row") * rows, rows)
    live_cols = lax.dynamic_slice_in_dim(live, lax.axis_index("ch") * cols, cols)
    mask = live_rows.reshape(2, half).T[:, :, None] * live_cols[None, None, :]
    f32, bf16 = jnp.float32, jnp.bfloat16
    vm = pltpu.VMEM
    zs = chs_n // 2
    reach = zs * cols
    part_h = own_h // CHUNKS
    scratch = [
        vm((total, chans), f32),
        vm((total, chans), f32),
        vm((total, chans), f32),
        vm((total, chans), bf16),
        vm((2, blocks, hidden, wide), f32),
        vm((2, blocks, hidden, wide), f32),
        vm((2 * (hidden // CHUNKS) * half, lanes), f32),
        vm((hidden * half, lanes), f32),
        vm((2 * hidden * half, lanes), f32),
        vm((own_h, side, reach), bf16),
        vm((own_h, side, reach), bf16),
        vm((1, side, side), bf16),
        vm((own_h, side, reach), f32),
        vm((blocks, hidden, wide), f32),
        vm((blocks, hidden, wide), bf16),
    ]
    edge_slots = vm((CHUNKS, peers, 2 * part_h, half, lanes), bf16)
    part_slots = vm((CHUNKS, part_h, side, reach), bf16)
    tri_slots = vm((CHUNKS, peers, part_h, half, lanes), bf16)
    both_slots = vm((CHUNKS, 2 * peers, part_h, half, lanes), bf16)
    scratch += [edge_slots, edge_slots, part_slots, part_slots, tri_slots, tri_slots]
    scratch += [tri_slots, both_slots, edge_slots, edge_slots]
    sems = pltpu.SemaphoreType.DMA((5, CHUNKS, 2 * peers))
    scratch += [sems, sems]
    whole = pl.BlockSpec(memory_space=pltpu.VMEM)
    out = jax.ShapeDtypeStruct((rows, cols, chans), bf16)
    return pl.pallas_call(
        functools.partial(fused_kernel, rows_n, chs_n),
        out_shape=(out, out),
        in_specs=[whole] * 8,
        out_specs=(whole, whole),
        scratch_shapes=scratch,
        compiler_params=pltpu.CompilerParams(
            collective_id=0, has_side_effects=True, vmem_limit_bytes=56 * 1024 * 1024
        ),
    )(
        pair_tensor,
        cotangent,
        mask.reshape(half, lanes),
        in_gain.reshape(1, chans),
        edge_weight.reshape(4, chans, peers, CHUNKS, part_h)
        .transpose(0, 3, 2, 4, 1)
        .reshape(4 * hidden, chans),
        gate_weight,
        out_gain.reshape(hidden, 1),
        out_weight,
    )


def solution(mesh):
    in_specs = (
        P(("grp", "row"), "ch", None),
        P(("grp", "row"), "ch", None),
        P("grp"),
        P(),
        P(),
        P(),
        P(),
        P(),
    )
    out_specs = (P(("grp", "row"), "ch", None), P(("grp", "row"), "ch", None))
    rows_n, chs_n = mesh.shape["row"], mesh.shape["ch"]
    body = per_device
    owners = rows_n * chs_n // 2
    if chs_n % 2 == 0 and 128 % (owners * CHUNKS) == 0:
        body = functools.partial(fused_device, rows_n, chs_n)
    return jax.shard_map(
        body, mesh=mesh, in_specs=in_specs, out_specs=out_specs, check_vma=False
    )
```
